32 devices in a mesh: row: 8 (over z, core), col: 4 (over y, x).
Axes of the slice: x: 2, y: 2, z: 4, core: 2. Of those that a mesh axis runs over, the one named last changes fastest.
Arguments:
- tokens: bfloat16 [1024, 12288], P('row', 'col'), may hold values from -6 to 6
- weight: bfloat16 [12288, 24576], P('col', 'row'), may hold values from -0.0546875 to 0.0546875
- cotangent: bfloat16 [1024, 24576], P('col', 'row'), may hold values from -6 to 6
Outputs:
- hidden: bfloat16 [1024, 24576], P('col', 'row')
- grad_weight: float32 [12288, 24576], P('col', 'row')
- grad_tokens: bfloat16 [1024, 12288], P('row', 'col')
The draws below stay inside these ranges and needn't reach their ends.
All inputs are finite; a program needn't handle non-finite values.
Results may differ from the reference program's by a relative error of at most 0.0049.
Values may be sent and summed in bfloat16 or wider, within the bound.
A program may use at most 192 MiB of HBM per device.

```python
import math
import jax
import jax.numpy as jnp
from jax import lax

D = 12288
F = 24576
TOKENS = 1024


def steps_of(rng, dims, cuts, least, high):
    level, own = 1.0, jax.random.fold_in(rng, 6)
    for dim, blocks in cuts:
        steps = jnp.exp(jax.random.uniform(jax.random.fold_in(own, dim), (blocks,), jnp.float32, least / len(cuts), high / len(cuts)))
        level = level * jnp.repeat(steps, dims[dim] // blocks).reshape([-1 if axis == dim else 1 for axis in range(len(dims))])
    return level


def scatter_about(own_key, shape, deviation, bound, pieces=(), dtype=jnp.bfloat16):
    result = deviation * jax.random.normal(own_key, shape, jnp.float32)
    if pieces:
        result = result * steps_of(own_key, shape, pieces, -0.22, 0.18)
    return jnp.clip(result, -bound, bound).astype(dtype)


def setup_inputs(seed: int = 0) -> dict:
    seeds = jax.random.split(jax.random.key(seed), 4)
    return {
        "tokens": scatter_about(seeds[0], (TOKENS, D), 1.0, 6.0, ((0, 8), (1, 4))),
        "weight": scatter_about(seeds[1], (D, F), D ** -0.5, 0.0546875, ((0, 4), (1, 8))),
        "cotangent": scatter_about(seeds[2], (TOKENS, F), 1.0, 6.0, ((0, 4), (1, 8))),
    }


def gelu_exact(value):
    return 0.5 * value * (1.0 + jax.scipy.special.erf(value / math.sqrt(2.0)))

def gelu_slope(value):
    cumulative = 0.5 * (1.0 + jax.scipy.special.erf(value / math.sqrt(2.0)))
    return cumulative + value * jnp.exp(-0.5 * value * value) / math.sqrt(2.0 * math.pi)

def reference(tokens, weight, cotangent):
    pre = jnp.dot(tokens, weight, preferred_element_type=jnp.float32)
    hidden = gelu_exact(pre).astype(jnp.bfloat16)
    grad_pre = (cotangent.astype(jnp.float32) * gelu_slope(pre)).astype(jnp.bfloat16)
    grad_weight = lax.dot_general(tokens, grad_pre, (((0,), (0,)), ((), ())), preferred_element_type=jnp.float32)
    grad_tokens = lax.dot_general(grad_pre, weight, (((1,), (1,)), ((), ())), preferred_element_type=jnp.float32)
    return (hidden, grad_weight, grad_tokens.astype(jnp.bfloat16))
```

```python
import math

import jax
import jax.numpy as jnp
from jax import lax
from jax.experimental import pallas as pl
from jax.experimental.pallas import tpu as pltpu
from jax.sharding import PartitionSpec as P

PARTS = 2


def gelu_exact(value):
    return 0.5 * value * (1.0 + jax.scipy.special.erf(value / math.sqrt(2.0)))


def gelu_slope(value):
    cumulative = 0.5 * (1.0 + jax.scipy.special.erf(value / math.sqrt(2.0)))
    return cumulative + value * jnp.exp(-0.5 * value * value) / math.sqrt(2.0 * math.pi)


def dot_t_kernel(a_ref, b_ref, out_ref):
    out_ref[...] = lax.dot_general(
        a_ref[...], b_ref[...], (((0,), (0,)), ((), ())), preferred_element_type=jnp.float32
    )


def dot_t(a, b):
    rows, m = a.shape
    n = b.shape[1]
    block = 256
    return pl.pallas_call(
        dot_t_kernel,
        grid=(m // block,),
        in_specs=[
            pl.BlockSpec((rows, block), lambda i: (0, i)),
            pl.BlockSpec((rows, n), lambda i: (0, 0)),
        ],
        out_specs=pl.BlockSpec((block, n), lambda i: (i, 0)),
        out_shape=jax.ShapeDtypeStruct((m, n), jnp.float32),
        compiler_params=pltpu.CompilerParams(vmem_limit_bytes=48 * 1024 * 1024),
        cost_estimate=pl.CostEstimate(
            flops=2 * rows * m * n,
            bytes_accessed=2 * rows * (m + n) + 4 * m * n,
            transcendentals=0,
        ),
    )(a, b)


def swap(value, bit):
    return lax.ppermute(value, "col", [(c, c ^ bit) for c in range(4)])


def pick(value, axis, index):
    return lax.dynamic_index_in_dim(value, index, axis, keepdims=False)


def ordered(mine, other, index, axis):
    first = jnp.where(index == 0, mine, other)
    second = jnp.where(index == 0, other, mine)
    return jnp.stack([first, second], axis)


def scatter_square(partial, x_first):
    me = lax.axis_index("col")
    x, y = me % 2, me // 2
    a = partial.reshape((2, 2) + partial.shape[1:])
    if x_first:
        got = swap(pick(a, 1, 1 - x).astype(jnp.bfloat16), 1)
        a = pick(a, 1, x) + got.astype(jnp.float32)
        got = swap(pick(a, 0, 1 - y).astype(jnp.bfloat16), 2)
        return pick(a, 0, y) + got.astype(jnp.float32)
    got = swap(pick(a, 0, 1 - y).astype(jnp.bfloat16), 2)
    a = pick(a, 0, y) + got.astype(jnp.float32)
    got = swap(pick(a, 0, 1 - x).astype(jnp.bfloat16), 1)
    return pick(a, 0, x) + got.astype(jnp.float32)


def gather_square(value, x_first):
    me = lax.axis_index("col")
    x, y = me % 2, me // 2
    if x_first:
        pair = ordered(value, swap(value, 1), x, 0)
        both = ordered(pair, swap(pair, 2), y, 0)
    else:
        pair = ordered(value, swap(value, 2), y, 0)
        both = ordered(pair, swap(pair, 1), x, 1)
    return both.reshape((4,) + value.shape)


def make(row_n, col_n):
    def shards(tokens, weight, cotangent):
        local, features = tokens.shape
        hidden_n = weight.shape[1]
        owned = cotangent.shape[0]
        sub = local // PARTS
        blocks = owned // local
        square = col_n == 4
        cuts = 2 if square else 1
        wide = hidden_n // cuts
        split = cotangent.reshape(blocks, PARTS, sub, hidden_n)

        gathered = [
            lax.all_gather(tokens[p * sub : (p + 1) * sub], "row", axis=0, tiled=True)
            for p in range(PARTS)
        ]
        hiddens, grads = [], []
        for p in range(PARTS):
            hs, gs = [], []
            for h in range(cuts):
                cols = slice(h * wide, (h + 1) * wide)
                partial = jnp.dot(
                    gathered[p], weight[:, cols], preferred_element_type=jnp.float32
                )
                if square:
                    pre = scatter_square(partial.reshape(col_n, blocks * sub, wide), h == 0)
                else:
                    pre = lax.psum_scatter(partial, "col", scatter_dimension=0, tiled=True)
                cot = split[:, p, :, cols].reshape(blocks * sub, wide)
                hs.append(gelu_exact(pre).astype(jnp.bfloat16))
                grad_pre = (cot.astype(jnp.float32) * gelu_slope(pre)).astype(jnp.bfloat16)
                if square:
                    part = gather_square(grad_pre, h == 0).reshape(-1, wide)
                else:
                    part = lax.all_gather(grad_pre, "col", axis=0, tiled=True)
                gs.append(part)
            hiddens.append(jnp.concatenate(hs, 1).reshape(blocks, sub, hidden_n))
            grads.append(jnp.concatenate(gs, 1))
        hidden = jnp.stack(hiddens, 1).reshape(owned, hidden_n)

        outs = []
        for p in range(PARTS):
            back = lax.dot_general(
                grads[p], weight, (((1,), (1,)), ((), ())), preferred_element_type=jnp.float32
            ).astype(jnp.bfloat16)
            if p == PARTS - 1:
                back, *grads = lax.optimization_barrier((back, *grads))
            outs.append(lax.psum_scatter(back, "row", scatter_dimension=0, tiled=True))
        grad_tokens = jnp.concatenate(outs, 0)
        grad_weight = dot_t(jnp.concatenate(gathered, 0), jnp.concatenate(grads, 0))
        return (hidden, grad_weight, grad_tokens)

    return shards


def solution(mesh):
    in_specs = (P("row", "col"), P("col", "row"), P("col", "row"))
    out_specs = (P("col", "row"), P("col", "row"), P("row", "col"))
    return jax.shard_map(
        make(mesh.shape["row"], mesh.shape["col"]),
        mesh=mesh,
        in_specs=in_specs,
        out_specs=out_specs,
        check_vma=False,
    )
```

```python
import math

import jax
import jax.numpy as jnp
from jax import lax
from jax.experimental import pallas as pl
from jax.experimental.pallas import tpu as pltpu
from jax.sharding import PartitionSpec as P

PARTS = 4


def gelu_exact(value):
    return 0.5 * value * (1.0 + jax.scipy.special.erf(value / math.sqrt(2.0)))


def gelu_slope(value):
    cumulative = 0.5 * (1.0 + jax.scipy.special.erf(value / math.sqrt(2.0)))
    return cumulative + value * jnp.exp(-0.5 * value * value) / math.sqrt(2.0 * math.pi)


def dot_parts_kernel(a_ref, *refs):
    parts, out_ref, held = refs[:-2], refs[-2], refs[-1]
    rows = parts[0].shape[0]

    @pl.when(pl.program_id(0) == 0)
    def _():
        for p, part in enumerate(parts):
            held[p * rows : (p + 1) * rows] = part[...]

    out_ref[...] = jnp.dot(a_ref[...], held[...], preferred_element_type=jnp.float32)


def dot_parts(a, parts):
    m, depth = a.shape
    rows, n = parts[0].shape
    block = 256
    return pl.pallas_call(
        dot_parts_kernel,
        grid=(m // block,),
        in_specs=[pl.BlockSpec((block, depth), lambda i: (i, 0))]
        + [pl.BlockSpec((rows, n), lambda i: (0, 0)) for _ in parts],
        out_specs=pl.BlockSpec((block, n), lambda i: (i, 0)),
        out_shape=jax.ShapeDtypeStruct((m, n), jnp.float32),
        scratch_shapes=[pltpu.VMEM((depth, n), jnp.bfloat16)],
        compiler_params=pltpu.CompilerParams(vmem_limit_bytes=48 * 1024 * 1024),
        cost_estimate=pl.CostEstimate(
            flops=2 * depth * m * n,
            bytes_accessed=2 * depth * (m + n) + 4 * m * n,
            transcendentals=0,
        ),
    )(a, *parts)


def swap(value, bit):
    return lax.ppermute(value, "col", [(c, c ^ bit) for c in range(4)])


def pick(value, axis, index):
    return lax.dynamic_index_in_dim(value, index, axis, keepdims=False)


def ordered(mine, other, index, axis):
    first = jnp.where(index == 0, mine, other)
    second = jnp.where(index == 0, other, mine)
    return jnp.stack([first, second], axis)


def scatter_first(partial, x_first):
    me = lax.axis_index("col")
    x, y = me % 2, me // 2
    a = partial.reshape((2, 2) + partial.shape[1:])
    axis, bit, at = (1, 1, x) if x_first else (0, 2, y)
    got = swap(pick(a, axis, 1 - at).astype(jnp.bfloat16), bit)
    return pick(a, axis, at) + got.astype(jnp.float32)


def scatter_second(a, x_first):
    me = lax.axis_index("col")
    bit, at = (2, me // 2) if x_first else (1, me % 2)
    got = swap(pick(a, 0, 1 - at).astype(jnp.bfloat16), bit)
    return pick(a, 0, at) + got.astype(jnp.float32)


def pair_sum(partial, n):
    core = lax.axis_index("row") % 2
    a = partial.reshape((n // 2, 2) + partial.shape[1:])
    got = lax.ppermute(
        pick(a, 1, 1 - core).astype(jnp.bfloat16), "row", [(r, r ^ 1) for r in range(n)]
    )
    return pick(a, 1, core) + got.astype(jnp.float32)


def scatter_z(a, n):
    z, nz = lax.axis_index("row") // 2, n // 2
    total = pick(a, 0, z)
    for k in range(1, nz):
        block = pick(a, 0, (z + k) % nz).astype(jnp.bfloat16)
        got = lax.ppermute(block, "row", [(r, (r + 2 * k) % n) for r in range(n)])
        total = total + got.astype(jnp.float32)
    return total.astype(jnp.bfloat16)


def gather_square(value, x_first):
    me = lax.axis_index("col")
    x, y = me % 2, me // 2
    if x_first:
        pair = ordered(value, swap(value, 1), x, 0)
        both = ordered(pair, swap(pair, 2), y, 0)
    else:
        pair = ordered(value, swap(value, 2), y, 0)
        both = ordered(pair, swap(pair, 1), x, 1)
    return both.reshape((4,) + value.shape)


def make(row_n, col_n):
    def shards(tokens, weight, cotangent):
        local, features = tokens.shape
        hidden_n = weight.shape[1]
        owned = cotangent.shape[0]
        sub = local // PARTS
        blocks = owned // local
        square = col_n == 4
        cuts = 2 if square else 1
        wide = hidden_n // cuts
        split = cotangent.reshape(blocks, PARTS, sub, hidden_n)

        gathered = [
            lax.all_gather(tokens[p * sub : (p + 1) * sub], "row", axis=0, tiled=True)
            for p in range(PARTS)
        ]
        hiddens, grads, outs = [], [], []
        for p in range(PARTS):
            rows, firsts = gathered[p], []
            if square and p:
                rows, *_ = lax.optimization_barrier((rows, *held))
            for h in range(cuts):
                cols = slice(h * wide, (h + 1) * wide)
                partial = jnp.dot(rows, weight[:, cols], preferred_element_type=jnp.float32)
                if square:
                    partial = partial.reshape(col_n, blocks * sub, wide)
                    firsts.append(scatter_first(partial, h == 0))
                else:
                    firsts.append(partial)
            held = firsts
            hs, gs = [], []
            for h in range(cuts):
                cols = slice(h * wide, (h + 1) * wide)
                if square:
                    pre = scatter_second(firsts[h], h == 0)
                else:
                    pre = lax.psum_scatter(firsts[h], "col", scatter_dimension=0, tiled=True)
                cot = split[:, p, :, cols].reshape(blocks * sub, wide)
                hs.append(gelu_exact(pre).astype(jnp.bfloat16))
                grad_pre = (cot.astype(jnp.float32) * gelu_slope(pre)).astype(jnp.bfloat16)
                if square:
                    part = gather_square(grad_pre, h == 0).reshape(-1, wide)
                else:
                    part = lax.all_gather(grad_pre, "col", axis=0, tiled=True)
                gs.append(part)
            hiddens.append(jnp.concatenate(hs, 1).reshape(blocks, sub, hidden_n))
            grad = jnp.concatenate(gs, 1)
            if p:
                grad, _ = lax.optimization_barrier((grad, pairs))
            back = lax.dot_general(
                grad, weight, (((1,), (1,)), ((), ())), preferred_element_type=jnp.float32
            )
            grads.append(grad)
            pairs = pair_sum(back.reshape(row_n, sub, features), row_n)
            if p == PARTS - 1:
                pairs, *grads = lax.optimization_barrier((pairs, *grads))
            outs.append(scatter_z(pairs, row_n))
        hidden = jnp.stack(hiddens, 1).reshape(owned, hidden_n)
        grad_tokens = jnp.concatenate(outs, 0)
        *gathered, _ = lax.optimization_barrier((*gathered, held[0]))
        turned = jnp.concatenate(gathered, 0).T
        grad_weight = dot_parts(turned, grads)
        return (hidden, grad_weight, grad_tokens)

    return shards


def solution(mesh):
    in_specs = (P("row", "col"), P("col", "row"), P("col", "row"))
    out_specs = (P("col", "row"), P("col", "row"), P("row", "col"))
    return jax.shard_map(
        make(mesh.shape["row"], mesh.shape["col"]),
        mesh=mesh,
        in_specs=in_specs,
        out_specs=out_specs,
        check_vma=False,
    )
```

```python
import math

import jax
import jax.numpy as jnp
from jax import lax
from jax.experimental import pallas as pl
from jax.experimental.pallas import tpu as pltpu
from jax.sharding import PartitionSpec as P

PARTS = 2


def gelu_exact(value):
    return 0.5 * value * (1.0 + jax.scipy.special.erf(value / math.sqrt(2.0)))


def gelu_slope(value):
    cumulative = 0.5 * (1.0 + jax.scipy.special.erf(value / math.sqrt(2.0)))
    return cumulative + value * jnp.exp(-0.5 * value * value) / math.sqrt(2.0 * math.pi)


def dot_parts_kernel(*refs):
    parts, out_ref = refs[:-1], refs[-1]
    half = len(parts) // 2
    total = None
    for a_ref, b_ref in zip(parts[:half], parts[half:]):
        term = lax.dot_general(
            a_ref[...], b_ref[...], (((0,), (0,)), ((), ())), preferred_element_type=jnp.float32
        )
        total = term if total is None else total + term
    out_ref[...] = total


def dot_parts(a, b):
    rows, m = a[0].shape
    n = b[0].shape[1]
    block = 256
    depth = rows * len(a)
    return pl.pallas_call(
        dot_parts_kernel,
        grid=(m // block,),
        in_specs=[pl.BlockSpec((rows, block), lambda i: (0, i)) for _ in a]
        + [pl.BlockSpec((rows, n), lambda i: (0, 0)) for _ in b],
        out_specs=pl.BlockSpec((block, n), lambda i: (i, 0)),
        out_shape=jax.ShapeDtypeStruct((m, n), jnp.float32),
        compiler_params=pltpu.CompilerParams(vmem_limit_bytes=48 * 1024 * 1024),
        cost_estimate=pl.CostEstimate(
            flops=2 * depth * m * n,
            bytes_accessed=2 * depth * (m + n) + 4 * m * n,
            transcendentals=0,
        ),
    )(*a, *b)


def swap(value, bit):
    return lax.ppermute(value, "col", [(c, c ^ bit) for c in range(4)])


def pick(value, axis, index):
    return lax.dynamic_index_in_dim(value, index, axis, keepdims=False)


def ordered(mine, other, index, axis):
    first = jnp.where(index == 0, mine, other)
    second = jnp.where(index == 0, other, mine)
    return jnp.stack([first, second], axis)


def scatter_first(partial, x_first):
    me = lax.axis_index("col")
    x, y = me % 2, me // 2
    a = partial.reshape((2, 2) + partial.shape[1:])
    axis, bit, at = (1, 1, x) if x_first else (0, 2, y)
    got = swap(pick(a, axis, 1 - at).astype(jnp.bfloat16), bit)
    return pick(a, axis, at) + got.astype(jnp.float32)


def scatter_second(a, x_first):
    me = lax.axis_index("col")
    bit, at = (2, me // 2) if x_first else (1, me % 2)
    got = swap(pick(a, 0, 1 - at).astype(jnp.bfloat16), bit)
    return pick(a, 0, at) + got.astype(jnp.float32)


def pair_sum(partial, n):
    core = lax.axis_index("row") % 2
    a = partial.reshape((n // 2, 2) + partial.shape[1:])
    got = lax.ppermute(
        pick(a, 1, 1 - core).astype(jnp.bfloat16), "row", [(r, r ^ 1) for r in range(n)]
    )
    return pick(a, 1, core) + got.astype(jnp.float32)


def scatter_z(a, n):
    z, nz = lax.axis_index("row") // 2, n // 2
    total = pick(a, 0, z)
    for k in range(1, nz):
        block = pick(a, 0, (z + k) % nz).astype(jnp.bfloat16)
        got = lax.ppermute(block, "row", [(r, (r + 2 * k) % n) for r in range(n)])
        total = total + got.astype(jnp.float32)
    return total.astype(jnp.bfloat16)


def behind(value, after):
    return lax.optimization_barrier((value, *after))[0]


def gather_square(value, x_first, after):
    me = lax.axis_index("col")
    x, y = me % 2, me // 2
    if x_first:
        pair = behind(ordered(value, swap(value, 1), x, 0), after)
        both = ordered(pair, swap(pair, 2), y, 0)
    else:
        pair = behind(ordered(value, swap(value, 2), y, 0), after)
        both = ordered(pair, swap(pair, 1), x, 1)
    return both.reshape((4,) + value.shape)


def make(row_n, col_n):
    def shards(tokens, weight, cotangent):
        local, features = tokens.shape
        hidden_n = weight.shape[1]
        owned = cotangent.shape[0]
        sub = local // PARTS
        blocks = owned // local
        square = col_n == 4
        cuts = 2 if square else 1
        wide = hidden_n // cuts
        split = cotangent.reshape(blocks, PARTS, sub, hidden_n)

        gathered = [
            lax.all_gather(tokens[p * sub : (p + 1) * sub], "row", axis=0, tiled=True)
            for p in range(PARTS)
        ]
        hiddens, grads, outs, sent = [], [], [], []
        for p in range(PARTS):
            rows, firsts = gathered[p], []
            if square and p:
                rows, *_ = lax.optimization_barrier((rows, *held))
            for h in range(cuts):
                cols = slice(h * wide, (h + 1) * wide)
                partial = jnp.dot(rows, weight[:, cols], preferred_element_type=jnp.float32)
                if square:
                    partial = partial.reshape(col_n, blocks * sub, wide)
                    firsts.append(scatter_first(partial, h == 0))
                else:
                    firsts.append(partial)
            held = firsts
            hs, gs = [], []
            for h in range(cuts):
                cols = slice(h * wide, (h + 1) * wide)
                if square:
                    pre = scatter_second(firsts[h], h == 0)
                else:
                    pre = lax.psum_scatter(firsts[h], "col", scatter_dimension=0, tiled=True)
                cot = split[:, p, :, cols].reshape(blocks * sub, wide)
                hs.append(gelu_exact(pre).astype(jnp.bfloat16))
                grad_pre = (cot.astype(jnp.float32) * gelu_slope(pre)).astype(jnp.bfloat16)
                if square:
                    part = gather_square(grad_pre, h == 0, sent).reshape(-1, wide)
                else:
                    part = lax.all_gather(grad_pre, "col", axis=0, tiled=True)
                gs.append(part)
            hiddens.append(jnp.concatenate(hs, 1).reshape(blocks, sub, hidden_n))
            grad = jnp.concatenate(gs, 1)
            back = lax.dot_general(
                grad, weight, (((1,), (1,)), ((), ())), preferred_element_type=jnp.float32
            )
            grads.append(grad)
            pairs = pair_sum(back.reshape(row_n, sub, features), row_n)
            if p == PARTS - 1:
                pairs, *grads = lax.optimization_barrier((pairs, *grads))
            sent = [pairs]
            outs.append(scatter_z(pairs, row_n))
        hidden = jnp.stack(hiddens, 1).reshape(owned, hidden_n)
        grad_tokens = jnp.concatenate(outs, 0)
        grad_weight = dot_parts(gathered, grads)
        return (hidden, grad_weight, grad_tokens)

    return shards


def solution(mesh):
    in_specs = (P("row", "col"), P("col", "row"), P("col", "row"))
    out_specs = (P("col", "row"), P("col", "row"), P("row", "col"))
    return jax.shard_map(
        make(mesh.shape["row"], mesh.shape["col"]),
        mesh=mesh,
        in_specs=in_specs,
        out_specs=out_specs,
        check_vma=False,
    )
```
